32 devices in a mesh: wide: 8 (over y, x, core), narrow: 4 (over z).
Axes of the slice: x: 2, y: 2, z: 4, core: 2. Of those that a mesh axis runs over, the one named last changes fastest.
Arguments:
- dosages: int32 [2048, 6144], P('narrow', 'wide'), may hold values from 0 to 3, as said below
- allele_counts: int32 [2048], P('narrow'), may hold values from 4000 to 384000, as said below
- called_counts: int32 [2048], P('narrow'), may hold values from 200000 to 400000
Outputs:
- relation: float32 [8, 4, 192, 6144], P(None, 'narrow', None, 'wide')
The draws below stay inside these ranges and needn't reach their ends.
Inputs may be any that keep to these rules, and one draw needn't show every extreme that they name: 3 marks a missing call; 0, 1 and 2 are dosages. `allele_counts`: the floor of the SNP's called_counts times a whole number p from 1 to 48, divided by 50, so that freq lies in (0, 0.5).
All inputs are finite; a program needn't handle non-finite values.
Results may differ from the reference program's by a relative error of at most 0.0043.
Values may be sent and summed in bfloat16 or wider, within the bound.
No kernel may reach another device: no remote copies, remote signals or barrier semaphores. Data moves between devices by JAX's collectives and lax.ppermute only.
A program may use at most 128 MiB of HBM per device.

```python
import jax
import jax.numpy as jnp
from jax import lax

SNPS = 2048
SUB = 192
COHORT = 400000
BLK = 768
SAMPLES = 6144
N_WIDE = 8
N_NARROW = 4


def cohort_counts(key):
    called_counts = jax.random.randint(jax.random.fold_in(key, 11), (SNPS,), COHORT // 2, COHORT + 1)
    percent = jax.random.randint(jax.random.fold_in(key, 12), (SNPS,), 1, 49)
    called_counts = called_counts.at[0].set(COHORT).at[1].set(COHORT // 2)
    percent = percent.at[0].set(48).at[1].set(1)
    allele_counts = called_counts * percent // 50
    return (called_counts, allele_counts)


def draw_allele_counts(key, part):
    return cohort_counts(key)[1].astype(jnp.int32)


def draw_called_counts(key, part):
    return cohort_counts(key)[0].astype(jnp.int32)


def draw_dosages(key, part):
    called_counts, allele_counts = cohort_counts(key)
    copies_top = (2 * called_counts)[:, None]
    first = jax.random.randint(jax.random.fold_in(key, 21), (SNPS, SAMPLES), 0, copies_top)
    second = jax.random.randint(jax.random.fold_in(key, 22), (SNPS, SAMPLES), 0, copies_top)
    dosage = (first < allele_counts[:, None]).astype(jnp.int32) + (second < allele_counts[:, None]).astype(jnp.int32)
    missing = jax.random.randint(jax.random.fold_in(key, 23), (SNPS, SAMPLES), 0, 20) == 0
    return jnp.where(missing, 3, dosage).astype(jnp.int32)


def setup_inputs(seed: int = 0) -> dict:
    arg_keys = jax.random.split(jax.random.key(seed), 4)
    return {
        "dosages": draw_dosages(jax.random.fold_in(arg_keys[3], 71), 0),
        "allele_counts": draw_allele_counts(jax.random.fold_in(arg_keys[3], 71), 0),
        "called_counts": draw_called_counts(jax.random.fold_in(arg_keys[3], 71), 0),
    }


def standardize(dosages, allele_counts, called_counts):
    freq = allele_counts.astype(jnp.float32) / (2.0 * called_counts.astype(jnp.float32))
    freq = freq[:, None]
    values = (dosages.astype(jnp.float32) - 2.0 * freq) * lax.rsqrt(2.0 * freq * (1.0 - freq))
    values = jnp.where(dosages == 3, jnp.zeros_like(values), values)
    return values.astype(jnp.bfloat16)

def reference(dosages, allele_counts, called_counts):
    standard = standardize(dosages, allele_counts, called_counts)
    blocks = jnp.transpose(standard.reshape(SNPS, N_WIDE, BLK), (1, 0, 2))

    def row_block(piece):
        product = lax.dot_general(piece, standard, (((0,), (0,)), ((), ())), preferred_element_type=jnp.float32)
        return product / SNPS
    grm = lax.map(row_block, blocks)
    return grm.reshape(N_WIDE, N_NARROW, SUB, SAMPLES)
```

```python
import functools

import jax
import jax.numpy as jnp
from jax import lax
from jax.experimental import pallas as pl
from jax.experimental.pallas import tpu as pltpu
from jax.sharding import PartitionSpec as P

PARTS = 2
LANES = 128
ANY = pl.BlockSpec(memory_space=pl.ANY)


def partners(z):
    side = lax.rem(z, 2)
    return z + 1 - 2 * side, z - 1 + 2 * side


def trade(value, odd, step):
    n = lax.axis_size("narrow")
    pairs = []
    for low in range(odd, n - 1, 2):
        if low + 1 - step >= 0:
            pairs.append((low, low + 1))
        if low + step <= n - 1:
            pairs.append((low + 1, low))
    return lax.ppermute(value, "narrow", pairs) if pairs else None


def slab_of(z, odd, step):
    side = lax.rem(z + odd, 2)
    return z + step * (1 - 2 * side)


def standardize_kernel(n, dosages, allele, called, own, *without):
    z = lax.axis_index("narrow")
    snps, cols = dosages.shape
    sub = cols // n
    part = snps // PARTS
    for start in range(0, snps, LANES):
        lanes = pl.ds(start, LANES)
        freq = allele[:, lanes].astype(jnp.float32) / (2.0 * called[:, lanes].astype(jnp.float32))
        scale = lax.rsqrt(2.0 * freq * (1.0 - freq))
        dose = dosages[lanes, :].astype(jnp.float32).T
        values = jnp.where(dose == 3.0, 0.0, (dose - 2.0 * freq) * scale).astype(jnp.bfloat16)
        own[:, lanes] = values
        h, rest = start // part, start % part
        for odd in range(2):
            other = jnp.clip(partners(z)[odd], 0, n - 1)
            ref = without[odd * PARTS + h]
            for q in range(n):
                slot = q - (q > other).astype(jnp.int32)

                @pl.when(q != other)
                def _(q=q, slot=slot, ref=ref):
                    rows = pl.ds(pl.multiple_of(slot * sub, sub), sub)
                    ref[rows, pl.ds(rest, LANES)] = values[q * sub : (q + 1) * sub]


def standardize(dosages, allele_counts, called_counts, n):
    snps, cols = dosages.shape
    sub = cols // n
    shapes = [jax.ShapeDtypeStruct((cols, snps), jnp.bfloat16)]
    shapes += [jax.ShapeDtypeStruct((cols - sub, snps // PARTS), jnp.bfloat16)] * (2 * PARTS)
    return pl.pallas_call(
        functools.partial(standardize_kernel, n),
        out_shape=shapes,
        compiler_params=pltpu.CompilerParams(vmem_limit_bytes=32 * 2**20),
        name="standardize",
    )(dosages, allele_counts[None], called_counts[None])


def multiply_kernel(n, wide, plan, keys, own, near, *refs):
    trades, panels = refs[: len(plan)], refs[len(plan) : len(plan) + wide]
    out, panel, block, tile, block_sem, panel_sem, out_sem = refs[len(plan) + wide :]
    z, w = lax.axis_index("narrow"), lax.axis_index("wide")
    cols, snps = own.shape
    sub = cols // n
    part = snps // PARTS

    def block_copies(act):
        def go(src, q, slab, h, width):
            rows = pl.ds(pl.multiple_of(q * sub, sub), sub)
            lanes = pl.ds(pl.multiple_of(slab * snps + h * part, LANES), width)
            act(pltpu.make_async_copy(src, block.at[rows, lanes], block_sem))

        for i in range(n):
            go(near.at[i], z, i, 0, snps)
        for q in range(n):
            pl.when(q != z)(lambda q=q: go(own.at[pl.ds(q * sub, sub), :], q, z, 0, snps))
        for ref, (odd, step, h) in zip(trades, plan):
            slab = slab_of(z, odd, step)
            other = partners(z)[odd]

            @pl.when((slab >= 0) & (slab < n) & (other >= 0) & (other < n))
            def _(ref=ref, slab=slab, h=h):
                for slot in range(n - 1):
                    go(ref.at[pl.ds(slot * sub, sub), :], slot + (slot >= z).astype(jnp.int32), slab, h, part)

    def panel_copies(t, act):
        for m in range(2):
            place = lax.rem(w ^ m, 2)
            rows = pl.ds(pl.multiple_of(place * sub, sub), sub)
            for i in range(n):
                act(pltpu.make_async_copy(
                    panels[2 * t + m].at[i], panel.at[t, rows, pl.ds(i * snps, snps)], panel_sem.at[t]))

    pairs = wide // 2
    block_copies(lambda copy: copy.start())
    for t in range(pairs):
        panel_copies(t, lambda copy: copy.start())
    block_copies(lambda copy: copy.wait())

    def out_copy(t):
        chip = (w ^ jnp.where(lax.rem(w, 2) == 0, *keys[t])) // 2
        rows = pl.ds(pl.multiple_of(chip * (2 * sub), 2 * sub), 2 * sub)
        return pltpu.make_async_copy(tile.at[t % 2], out.at[rows], out_sem.at[t % 2])

    for t in range(pairs):
        panel_copies(t, lambda copy: copy.wait())
        if t >= 2:
            out_copy(t - 2).wait()
        product = lax.dot_general(
            panel[t], block[...], (((1,), (1,)), ((), ())), preferred_element_type=jnp.float32
        )
        tile[t % 2] = product / (n * snps)
        out_copy(t).start()
    for t in range(max(pairs - 2, 0), pairs):
        out_copy(t).wait()


def multiply(own, near, trades, plan, panels, keys, n, wide):
    cols, snps = own.shape
    sub = cols // n
    return pl.pallas_call(
        functools.partial(multiply_kernel, n, wide, plan, keys),
        out_shape=jax.ShapeDtypeStruct((wide * sub, cols), jnp.float32),
        in_specs=[ANY] * (2 + len(trades) + len(panels)),
        out_specs=ANY,
        scratch_shapes=[
            pltpu.VMEM((wide // 2, 2 * sub, n * snps), jnp.bfloat16),
            pltpu.VMEM((cols, n * snps), jnp.bfloat16),
            pltpu.VMEM((2, 2 * sub, cols), jnp.float32),
            pltpu.SemaphoreType.DMA,
            pltpu.SemaphoreType.DMA((wide // 2,)),
            pltpu.SemaphoreType.DMA((2,)),
        ],
        compiler_params=pltpu.CompilerParams(vmem_limit_bytes=48 * 2**20),
        name="multiply",
    )(own, near, *trades, *panels)


def flip(value, masks):
    size = lax.axis_size("wide")
    return lax.ppermute(value, "wide", [(i, i ^ masks[i & 1]) for i in range(size)])


def spread(panel):
    size = lax.axis_size("wide")
    bits = [1 << b for b in range(1, size.bit_length() - 1)]
    got = {(0, 0): panel}
    for i in range(len(bits)):
        masks = (bits[i], bits[-1 - i])
        for key, value in list(got.items()):
            got[key[0] ^ masks[0], key[1] ^ masks[1]] = flip(value, masks)
    return got


def shards(dosages, allele_counts, called_counts):
    n, wide = lax.axis_size("narrow"), lax.axis_size("wide")
    z, w = lax.axis_index("narrow"), lax.axis_index("wide")
    snps, cols = dosages.shape
    sub = cols // n
    part = snps // PARTS
    own, *without = standardize(dosages, allele_counts, called_counts, n)
    near = lax.all_to_all(own.reshape(n, sub, snps), "narrow", 0, 0)

    def hand_on(value, odd, step, h):
        slab = jnp.clip(slab_of(z, odd, step), 0, n - 1)
        mine = lax.dynamic_slice(near, (slab, 0, h * part), (1, sub, part))[0]
        slot = jnp.clip(jnp.minimum(z, partners(z)[1 - odd]), 0, n - 2)
        return lax.dynamic_update_slice(value, mine, (slot * sub, 0))

    got = {}
    for step in range(1, n):
        for h in range(PARTS):
            for odd in range(2):
                if step == 1:
                    value = without[odd * PARTS + h]
                elif (1 - odd, step - 1, h) in got:
                    value = hand_on(got[1 - odd, step - 1, h], 1 - odd, step - 1, h)
                else:
                    continue
                value = trade(value, odd, step)
                if value is not None:
                    got[odd, step, h] = value
    plan = tuple(got)
    held = spread(near)
    partner = {key: flip(value, (1, 1)) for key, value in held.items()}
    keys = tuple(held)
    panels = [array for key in keys for array in (held[key], partner[key[::-1]])]
    result = multiply(own, near, [got[k] for k in plan], plan, panels, keys, n, wide)
    return result.reshape(wide, 1, sub, cols)


def solution(mesh):
    return jax.shard_map(
        shards,
        mesh=mesh,
        in_specs=(P("narrow", "wide"), P("narrow"), P("narrow")),
        out_specs=P(None, "narrow", None, "wide"),
        check_vma=False,
    )
```

```python
import functools
import math

import jax
import jax.numpy as jnp
from jax import lax
from jax.experimental import pallas as pl
from jax.experimental.pallas import tpu as pltpu
from jax.sharding import PartitionSpec as P

LANES = 128
HOP = 6_000_000_000
STACK = 0
EARLY = 6_000_000_000
ANY = pl.BlockSpec(memory_space=pl.ANY)
VMEM = pl.BlockSpec(memory_space=pltpu.VMEM)


def trade(value, swapped, step):
    n, wide = lax.axis_size("narrow"), lax.axis_size("wide")
    pairs = []
    for w in range(wide):
        for low in range((w + swapped) % 2, n - 1, 2):
            if low + 1 - step >= 0:
                pairs.append((w * n + low, w * n + low + 1))
            if low + step <= n - 1:
                pairs.append((w * n + low + 1, w * n + low))
    return lax.ppermute(value, ("wide", "narrow"), pairs)


def side_of(swapped):
    return lax.rem(lax.axis_index("wide") + swapped, 2)


def partner_on(z, odd):
    side = lax.rem(z + odd, 2)
    return z + 1 - 2 * side


def swap(value, mask):
    n = lax.axis_size("narrow")
    return lax.ppermute(value, "narrow", [(i, i ^ mask) for i in range(n)])


def slab_of(z, odd, step):
    side = lax.rem(z + odd, 2)
    return z + step * (1 - 2 * side)


def standardize_kernel(n, dosages_ref, allele_ref, called_ref, own, *refs):
    hops, panels, (dosages, allele, called, sem) = refs[:2], refs[2 : n + 1], refs[n + 1 :]
    z = lax.axis_index("narrow")
    snps, cols = dosages.shape
    sub = cols // n
    counts = [
        pltpu.make_async_copy(allele_ref, allele, sem.at[0]),
        pltpu.make_async_copy(called_ref, called, sem.at[1]),
    ]
    starts = range(0, snps, LANES)
    doses = [
        pltpu.make_async_copy(dosages_ref.at[pl.ds(start, LANES), :], dosages.at[pl.ds(start, LANES), :], sem.at[2 + i])
        for i, start in enumerate(starts)
    ]
    for copy in counts + doses:
        copy.start()
    for copy in counts:
        copy.wait()

    def put(values, ref, start, other):
        for q in range(n):
            slot = q - (q > other).astype(jnp.int32)

            @pl.when(q != other)
            def _():
                rows = pl.ds(pl.multiple_of(slot * sub, sub), sub)
                ref[rows, pl.ds(start, LANES)] = values[q * sub : (q + 1) * sub]

    for i, start in enumerate(starts):
        doses[i].wait()
        lanes = pl.ds(start, LANES)
        freq = allele[:, lanes].astype(jnp.float32) / (2.0 * called[:, lanes].astype(jnp.float32))
        scale = lax.rsqrt(2.0 * freq * (1.0 - freq))
        dose = dosages[lanes, :].astype(jnp.float32).T
        values = jnp.where(dose == 3.0, 0.0, (dose - 2.0 * freq) * scale).astype(jnp.bfloat16)
        own[:, lanes] = values
        for swapped, ref in enumerate(hops):
            put(values, ref, start, jnp.clip(partner_on(z, side_of(swapped)), 0, n - 1))
    for m, ref in enumerate(panels, 1):
        ref[...] = own[pl.ds(pl.multiple_of((z ^ m) * sub, sub), sub), :]


def standardize(dosages, allele_counts, called_counts, n):
    snps, cols = dosages.shape
    sub = cols // n
    shapes = [(cols, snps)] + [(cols - sub, snps)] * 2 + [(sub, snps)] * (n - 1)
    outs = pl.pallas_call(
        functools.partial(standardize_kernel, n),
        out_shape=[jax.ShapeDtypeStruct(shape, jnp.bfloat16) for shape in shapes],
        in_specs=[pl.BlockSpec(memory_space=pltpu.HBM)] * 3,
        scratch_shapes=[
            pltpu.VMEM((snps, cols), jnp.int32),
            pltpu.VMEM((1, snps), jnp.int32),
            pltpu.VMEM((1, snps), jnp.int32),
            pltpu.SemaphoreType.DMA((2 + snps // LANES,)),
        ],
        compiler_params=pltpu.CompilerParams(vmem_limit_bytes=60 * 2**20),
        name="standardize",
    )(dosages, allele_counts[None], called_counts[None])
    return outs[0], outs[1:3], outs[3:]


def stack_kernel(n, own, *refs):
    pieces, out = refs[: n - 1], refs[n - 1]
    z = lax.axis_index("narrow")
    sub = own.shape[0] // n
    out[z] = own[pl.ds(pl.multiple_of(z * sub, sub), sub), :]
    for m, piece in enumerate(pieces, 1):
        out[z ^ m] = piece[...]


def stack(own, pieces):
    n = len(pieces) + 1
    return pl.pallas_call(
        functools.partial(stack_kernel, n),
        out_shape=jax.ShapeDtypeStruct((n, own.shape[0] // n, own.shape[1]), own.dtype),
        compiler_params=pltpu.CompilerParams(vmem_limit_bytes=8 * 2**20),
        cost_estimate=pl.CostEstimate(flops=STACK, bytes_accessed=0, transcendentals=0),
        name="stack",
    )(own, *pieces)


def hand_on_kernel(n, step, first, second, near, *outs):
    z, sub = lax.axis_index("narrow"), near.shape[1]
    for swapped, value, out in ((1, second, outs[0]), (0, first, outs[1])):
        odd = side_of(swapped)
        slab = jnp.clip(slab_of(z, odd, step), 0, n - 1)
        to = jnp.clip(jnp.minimum(z, partner_on(z, 1 - odd)), 0, n - 2)
        out[...] = value[...]
        out[pl.ds(pl.multiple_of(to * sub, sub), sub), :] = near[slab]


def hand_on(first, second, near, step):
    n = near.shape[0]
    return pl.pallas_call(
        functools.partial(hand_on_kernel, n, step),
        out_shape=[jax.ShapeDtypeStruct(first.shape, first.dtype)] * 2,
        compiler_params=pltpu.CompilerParams(vmem_limit_bytes=12 * 2**20),
        cost_estimate=pl.CostEstimate(flops=HOP, bytes_accessed=0, transcendentals=0),
        name="hand_on",
    )(first, second, near)


def last_slab(z, n):
    return jnp.where(z < n // 2, n - 1, 0)


def block_copies(n, plan, own, near, trades, z, go):
    sub = near.shape[1]
    for i in range(n):
        go(near.at[i], z, i)
    if own is not None:
        for q in range(n):
            pl.when(q != z)(lambda q=q: go(own.at[pl.ds(q * sub, sub), :], q, z))
    for ref, (swapped, step) in zip(trades, plan):
        slab, other = slab_of(z, side_of(swapped), step), partner_on(z, side_of(swapped))

        @pl.when((slab >= 0) & (slab < n) & (other >= 0) & (other < n))
        def _(ref=ref, slab=slab):
            for slot in range(n - 1):
                go(ref.at[pl.ds(slot * sub, sub), :], slot + (slot >= z).astype(jnp.int32), slab)


def panel_rows(m, w, sub):
    return pl.ds(pl.multiple_of((m // 2 * 2 + (w + m) % 2) * sub, sub), sub)


def early_kernel(n, plan, own, near, *refs):
    trades, (*panels, out, rest, block, panel, tile, out_sem) = refs[: len(plan)], refs[len(plan) :]
    z, w = lax.axis_index("narrow"), lax.axis_index("wide")
    cols, snps = own.shape
    sub = cols // n
    last = last_slab(z, n)

    def place(slab):
        index = slab - (slab > last).astype(jnp.int32)
        return pl.ds(pl.multiple_of(index * snps, snps), snps)

    def go(src, q, slab):
        @pl.when(slab != last)
        def _():
            block[pl.ds(pl.multiple_of(q * sub, sub), sub), place(slab)] = src[...]

    block_copies(n, plan, own, near, trades, z, go)
    for m, ref in enumerate(panels):
        rows = panel_rows(m, w, sub)
        rest[rows, :] = ref[last]
        for i in range(n):

            @pl.when(i != last)
            def _(i=i, ref=ref, rows=rows):
                panel[rows, place(i)] = ref[i]

    width = tile.shape[2]
    outs = [
        pltpu.make_async_copy(tile.at[i % 2], out.at[:, pl.ds(start, width)], out_sem.at[i % 2])
        for i, start in enumerate(range(0, cols, width))
    ]
    for i, copy in enumerate(outs):
        if i >= 2:
            outs[i - 2].wait()
        tile[i % 2] = lax.dot_general(
            panel[...], block[pl.ds(i * width, width), :], (((1,), (1,)), ((), ())), preferred_element_type=jnp.float32
        )
        copy.start()
    for copy in outs[-2:]:
        copy.wait()


def late_kernel(n, plan, keys, near, early, rest, begun, first, second, *refs):
    trades, (out, block, panel, tile, out_sem) = refs[: len(plan)], refs[len(plan) :]
    z, w = lax.axis_index("narrow"), lax.axis_index("wide")
    cols, snps = block.shape
    sub = cols // n
    last = last_slab(z, n)
    dims = (((1,), (1,)), ((), ()))

    def out_copy(t):
        chip = (w ^ jnp.where(lax.rem(w, 2) == 0, *keys[t])) // 2
        rows = pl.ds(pl.multiple_of(chip * (2 * sub), 2 * sub), 2 * sub)
        return pltpu.make_async_copy(tile.at[t % 2], out.at[rows], out_sem.at[t % 2])

    def go(src, q, slab):
        @pl.when(slab == last)
        def _():
            block[pl.ds(pl.multiple_of(q * sub, sub), sub), :] = src[...]

    for m, ref in enumerate((first, second)):
        rows = panel_rows(m, w, sub)
        panel[rows, pl.ds((n - 1) * snps, snps)] = ref[last]
        for i in range(n):

            @pl.when(i != last)
            def _(i=i, ref=ref, rows=rows):
                index = i - (i > last).astype(jnp.int32)
                panel[rows, pl.ds(pl.multiple_of(index * snps, snps), snps)] = ref[i]

    block_copies(n, plan, None, near, trades, z, go)
    order = [len(keys) - 1, *range(len(keys) - 1)]
    for i, t in enumerate(order):
        if i >= 2:
            out_copy(order[i - 2]).wait()
        if i == 0:
            before = lax.dot_general(
                panel[:, : (n - 1) * snps], begun[...], dims, preferred_element_type=jnp.float32
            )
            left = panel[:, (n - 1) * snps :]
        else:
            rows = pl.ds(t * 2 * sub, 2 * sub)
            before, left = early[rows, :], rest[rows, :]
        product = lax.dot_general(left, block[...], dims, preferred_element_type=jnp.float32)
        tile[t % 2] = (before + product) / (n * snps)
        out_copy(t).start()
    for t in order[-2:]:
        out_copy(t).wait()


def limit(arrays):
    return min(sum(math.prod(a.shape) * a.dtype.itemsize for a in arrays) + 4 * 2**20, 60 * 2**20)


def multiply(own, near, got, panels, keys):
    n, sub, snps = near.shape
    rows, cols = (len(panels) - 2) * sub, own.shape[0]
    plan = tuple(key for key in got if key[1] < n - 1)
    width = 256 if cols % 256 == 0 else cols
    scratch = [
        pltpu.VMEM((rows, (n - 1) * snps), jnp.bfloat16),
        pltpu.VMEM((2, rows, width), jnp.float32),
    ]
    operands = [own, near, *[got[key] for key in plan], *panels[:-2]]
    outs = [
        jax.ShapeDtypeStruct((rows, cols), jnp.float32),
        jax.ShapeDtypeStruct((rows, snps), jnp.bfloat16),
        jax.ShapeDtypeStruct((cols, (n - 1) * snps), jnp.bfloat16),
    ]
    early = pl.pallas_call(
        functools.partial(early_kernel, n, plan),
        out_shape=outs,
        in_specs=[VMEM] * len(operands),
        out_specs=[ANY, VMEM, VMEM],
        scratch_shapes=scratch + [pltpu.SemaphoreType.DMA((2,))],
        compiler_params=pltpu.CompilerParams(vmem_limit_bytes=limit([*operands, *scratch, *outs[1:]])),
        cost_estimate=pl.CostEstimate(flops=EARLY, bytes_accessed=0, transcendentals=0),
        name="early",
    )(*operands)
    plan = tuple(key for key in got if key[1] >= n // 2)
    operands = [near, *early, *panels[-2:], *[got[key] for key in plan]]
    scratch = [
        pltpu.VMEM((cols, snps), jnp.bfloat16),
        pltpu.VMEM((2 * sub, n * snps), jnp.bfloat16),
        pltpu.VMEM((2, 2 * sub, cols), jnp.float32),
    ]
    return pl.pallas_call(
        functools.partial(late_kernel, n, plan, keys),
        out_shape=jax.ShapeDtypeStruct((len(panels) * sub, cols), jnp.float32),
        in_specs=[VMEM] * len(operands),
        out_specs=ANY,
        scratch_shapes=scratch + [pltpu.SemaphoreType.DMA((2,))],
        compiler_params=pltpu.CompilerParams(vmem_limit_bytes=limit([*operands, *scratch])),
        name="late",
    )(*operands)


def after(value, *earlier):
    return lax.optimization_barrier((value, *earlier))[0]


def flip(value, masks):
    size = lax.axis_size("wide")
    return lax.ppermute(value, "wide", [(i, i ^ masks[i & 1]) for i in range(size)])


def spread(panel):
    size = lax.axis_size("wide")
    bits = [1 << b for b in range(1, size.bit_length() - 1)]
    got = {(0, 0): panel}
    for i in range(len(bits)):
        masks = (bits[i], bits[-1 - i])
        for key, value in list(got.items()):
            got[key[0] ^ masks[0], key[1] ^ masks[1]] = flip(value, masks)
    return got


def shards(dosages, allele_counts, called_counts):
    n, wide = lax.axis_size("narrow"), lax.axis_size("wide")
    z, w = lax.axis_index("narrow"), lax.axis_index("wide")
    snps, cols = dosages.shape
    sub = cols // n
    own, hops, panels = standardize(dosages, allele_counts, called_counts, n)
    pieces = [swap(value, m) for m, value in enumerate(panels, 1)]
    near = stack(own, pieces)
    got = {(swapped, 1): trade(value, swapped, 1) for swapped, value in enumerate(hops)}
    for step in range(2, n):
        values = hand_on(got[0, step - 1], got[1, step - 1], near, step - 1)
        for swapped, value in enumerate(values):
            got[swapped, step] = trade(value, swapped, step)
    held = spread(near)
    partner = {key: flip(value, (1, 1)) for key, value in held.items()}
    keys = tuple(held)
    panels = [array for key in keys for array in (held[key], partner[key[::-1]])]
    result = multiply(own, near, got, panels, keys)
    return result.reshape(wide, 1, sub, cols)


def solution(mesh):
    return jax.shard_map(
        shards,
        mesh=mesh,
        in_specs=(P("narrow", "wide"), P("narrow"), P("narrow")),
        out_specs=P(None, "narrow", None, "wide"),
        check_vma=False,
    )
```

```python
import functools
import math

import jax
import jax.numpy as jnp
from jax import lax
from jax.experimental import pallas as pl
from jax.experimental.pallas import tpu as pltpu
from jax.sharding import PartitionSpec as P

LANES = 128
HOP = 20_000_000_000
PACE = 10_000_000_000
EARLY = 12_000_000_000
ANY = pl.BlockSpec(memory_space=pl.ANY)
VMEM = pl.BlockSpec(memory_space=pltpu.VMEM)
HBM = pl.BlockSpec(memory_space=pltpu.HBM)


def trade(value, swapped, step):
    n, wide = lax.axis_size("narrow"), lax.axis_size("wide")
    pairs = []
    for w in range(wide):
        for low in range((w + swapped) % 2, n - 1, 2):
            if low + 1 - step >= 0:
                pairs.append((w * n + low, w * n + low + 1))
            if low + step <= n - 1:
                pairs.append((w * n + low + 1, w * n + low))
    return lax.ppermute(value, ("wide", "narrow"), pairs)


def side_of(swapped):
    return lax.rem(lax.axis_index("wide") + swapped, 2)


def partner_on(z, odd):
    side = lax.rem(z + odd, 2)
    return z + 1 - 2 * side


def far_swap(value, mask):
    pairs = [(i, i ^ mask) for i in range(lax.axis_size("narrow"))]
    return lax.ppermute(value, "narrow", [(i, j) for i, j in pairs if abs(i - j) > 1])


def slab_of(z, odd, step):
    side = lax.rem(z + odd, 2)
    return z + step * (1 - 2 * side)


def standardize_kernel(n, dosages_ref, allele_ref, called_ref, own, *refs):
    panels, (dosages, allele, called, sem) = refs[: n - 2], refs[n - 2 :]
    z = lax.axis_index("narrow")
    snps, cols = dosages.shape
    sub = cols // n
    counts = [
        pltpu.make_async_copy(allele_ref, allele, sem.at[0]),
        pltpu.make_async_copy(called_ref, called, sem.at[1]),
    ]
    starts = range(0, snps, LANES)
    doses = [
        pltpu.make_async_copy(dosages_ref.at[pl.ds(start, LANES), :], dosages.at[pl.ds(start, LANES), :], sem.at[2 + i])
        for i, start in enumerate(starts)
    ]
    for copy in counts + doses:
        copy.start()
    for copy in counts:
        copy.wait()

    for i, start in enumerate(starts):
        doses[i].wait()
        lanes = pl.ds(start, LANES)
        freq = allele[:, lanes].astype(jnp.float32) / (2.0 * called[:, lanes].astype(jnp.float32))
        scale = lax.rsqrt(2.0 * freq * (1.0 - freq))
        dose = dosages[lanes, :].astype(jnp.float32).T
        values = jnp.where(dose == 3.0, 0.0, (dose - 2.0 * freq) * scale).astype(jnp.bfloat16)
        own[:, lanes] = values
    for m, ref in enumerate(panels, 2):
        ref[...] = own[pl.ds(pl.multiple_of((z ^ m) * sub, sub), sub), :]


def standardize(dosages, allele_counts, called_counts, n):
    snps, cols = dosages.shape
    sub = cols // n
    shapes = [(cols, snps)] + [(sub, snps)] * (n - 2)
    outs = pl.pallas_call(
        functools.partial(standardize_kernel, n),
        out_shape=[jax.ShapeDtypeStruct(shape, jnp.bfloat16) for shape in shapes],
        in_specs=[pl.BlockSpec(memory_space=pltpu.HBM)] * 3,
        scratch_shapes=[
            pltpu.VMEM((snps, cols), jnp.int32),
            pltpu.VMEM((1, snps), jnp.int32),
            pltpu.VMEM((1, snps), jnp.int32),
            pltpu.SemaphoreType.DMA((2 + snps // LANES,)),
        ],
        compiler_params=pltpu.CompilerParams(vmem_limit_bytes=60 * 2**20),
        name="standardize",
    )(dosages, allele_counts[None], called_counts[None])
    return outs[0], outs[1:]


def pick_kernel(own, out, sem):
    sub = out.shape[0]
    rows = pl.ds(pl.multiple_of(lax.axis_index("narrow") * sub, sub), sub)
    copy = pltpu.make_async_copy(own.at[rows, :], out, sem)
    copy.start()
    copy.wait()


def pick(own, sub):
    return pl.pallas_call(
        pick_kernel,
        out_shape=jax.ShapeDtypeStruct((sub, own.shape[1]), own.dtype),
        in_specs=[ANY],
        out_specs=VMEM,
        scratch_shapes=[pltpu.SemaphoreType.DMA],
        name="pick",
    )(own)


def stack_kernel(n, mine, first, second, *refs):
    pieces, out, sem = refs[: n - 2], refs[n - 2], refs[n - 1]
    z = lax.axis_index("narrow")
    sub = out.shape[1]
    rows = pl.ds(pl.multiple_of(z * sub, sub), sub)

    def hops(act):
        for swapped, value in enumerate((first, second)):
            other = partner_on(z, side_of(swapped))

            @pl.when((other >= 0) & (other < n))
            def _(swapped=swapped, value=value, other=other):
                act(pltpu.make_async_copy(value.at[rows, :], out.at[other], sem.at[swapped]))

    hops(lambda copy: copy.start())
    out[z] = mine[...]
    for m, piece in enumerate(pieces, 2):

        @pl.when(jnp.abs((z ^ m) - z) > 1)
        def _(m=m, piece=piece):
            out[z ^ m] = piece[...]

    hops(lambda copy: copy.wait())


def stack(mine, first, second, pieces):
    n = len(pieces) + 2
    return pl.pallas_call(
        functools.partial(stack_kernel, n),
        out_shape=jax.ShapeDtypeStruct((n, *mine.shape), mine.dtype),
        in_specs=[VMEM, ANY, ANY] + [VMEM] * (n - 2),
        out_specs=VMEM,
        scratch_shapes=[pltpu.SemaphoreType.DMA((2,))],
        compiler_params=pltpu.CompilerParams(vmem_limit_bytes=10 * 2**20),
        name="stack",
    )(mine, first, second, *pieces)


def hand_on_kernel(n, step, first, second, near, *outs):
    z, sub = lax.axis_index("narrow"), near.shape[1]
    for swapped, value, out in ((1, second, outs[0]), (0, first, outs[1])):
        odd = side_of(swapped)
        to = jnp.clip(partner_on(z, 1 - odd), 0, n - 1)
        if step == 1:
            for slot in range(n - 1):
                q = slot + (slot >= to).astype(jnp.int32)
                out[pl.ds(slot * sub, sub), :] = value[pl.ds(pl.multiple_of(q * sub, sub), sub), :]
        else:
            out[...] = value[...]
            slab = jnp.clip(slab_of(z, odd, step), 0, n - 1)
            slot = jnp.minimum(jnp.minimum(z, to), n - 2)
            out[pl.ds(pl.multiple_of(slot * sub, sub), sub), :] = near[slab]


def hand_on(first, second, near, step):
    n, sub, snps = near.shape
    return pl.pallas_call(
        functools.partial(hand_on_kernel, n, step),
        out_shape=[jax.ShapeDtypeStruct(((n - 1) * sub, snps), first.dtype)] * 2,
        compiler_params=pltpu.CompilerParams(vmem_limit_bytes=12 * 2**20),
        cost_estimate=pl.CostEstimate(flops=HOP, bytes_accessed=0, transcendentals=0),
        name="hand_on",
    )(first, second, near)


def last_slab(z, n):
    return jnp.where(z < n // 2, n - 1, 0)


def block_copies(n, plan, near, trades, z, go):
    sub = near.shape[1]
    for i in range(n):
        go(near.at[i], z, i)
    for ref, (swapped, step) in zip(trades, plan):
        slab, other = slab_of(z, side_of(swapped), step), partner_on(z, side_of(swapped))

        @pl.when((slab >= 0) & (slab < n) & (other >= 0) & (other < n))
        def _(ref=ref, slab=slab, step=step):
            if step == 1:
                for q in range(n):
                    pl.when(q != z)(lambda q=q: go(ref.at[pl.ds(q * sub, sub), :], q, slab))
            else:
                for slot in range(n - 1):
                    go(ref.at[pl.ds(slot * sub, sub), :], slot + (slot >= z).astype(jnp.int32), slab)


def panel_rows(m, w, sub):
    return pl.ds(pl.multiple_of((m // 2 * 2 + (w + m) % 2) * sub, sub), sub)


def early_kernel(n, plan, own, near, *refs):
    trades, (*panels, out, rest, block, panel, tile, own_sem, out_sem) = refs[: len(plan)], refs[len(plan) :]
    z, w = lax.axis_index("narrow"), lax.axis_index("wide")
    cols, snps = own.shape
    sub = cols // n
    last = last_slab(z, n)

    def place(slab):
        index = slab - (slab > last).astype(jnp.int32)
        return pl.ds(pl.multiple_of(index * snps, snps), snps)

    def go(src, q, slab):
        @pl.when(slab != last)
        def _():
            block[pl.ds(pl.multiple_of(q * sub, sub), sub), place(slab)] = src[...]

    def own_copies(act):
        for q in range(n):
            rows = pl.ds(q * sub, sub)

            @pl.when(q != z)
            def _(rows=rows):
                act(pltpu.make_async_copy(own.at[rows, :], block.at[rows, place(z)], own_sem))

    own_copies(lambda copy: copy.start())
    block_copies(n, plan, near, trades, z, go)
    for m, ref in enumerate(panels):
        rows = panel_rows(m, w, sub)
        rest[rows, :] = ref[last]
        for i in range(n):

            @pl.when(i != last)
            def _(i=i, ref=ref, rows=rows):
                panel[rows, place(i)] = ref[i]

    own_copies(lambda copy: copy.wait())
    width = tile.shape[2]
    outs = [
        pltpu.make_async_copy(tile.at[i % 2], out.at[:, pl.ds(start, width)], out_sem.at[i % 2])
        for i, start in enumerate(range(0, cols, width))
    ]
    for i, copy in enumerate(outs):
        if i >= 2:
            outs[i - 2].wait()
        tile[i % 2] = lax.dot_general(
            panel[...], block[pl.ds(i * width, width), :], (((1,), (1,)), ((), ())), preferred_element_type=jnp.float32
        )
        copy.start()
    for copy in outs[-2:]:
        copy.wait()


def last_block_kernel(n, plan, near, *refs):
    trades, block = refs[:-1], refs[-1]
    z, sub = lax.axis_index("narrow"), near.shape[1]
    last = last_slab(z, n)

    def go(src, q, slab):
        @pl.when(slab == last)
        def _():
            block[pl.ds(pl.multiple_of(q * sub, sub), sub), :] = src[...]

    block_copies(n, plan, near, trades, z, go)


def late_kernel(n, keys, block, early, rest, begun, first, second, out, panel, tile, out_sem):
    z, w = lax.axis_index("narrow"), lax.axis_index("wide")
    cols, snps = block.shape
    sub = cols // n
    last = last_slab(z, n)
    dims = (((1,), (1,)), ((), ()))

    def out_copy(t):
        chip = (w ^ jnp.where(lax.rem(w, 2) == 0, *keys[t])) // 2
        rows = pl.ds(pl.multiple_of(chip * (2 * sub), 2 * sub), 2 * sub)
        return pltpu.make_async_copy(tile.at[t % 2], out.at[rows], out_sem.at[t % 2])

    for m, ref in enumerate((first, second)):
        rows = panel_rows(m, w, sub)
        panel[rows, pl.ds((n - 1) * snps, snps)] = ref[last]
        for i in range(n):

            @pl.when(i != last)
            def _(i=i, ref=ref, rows=rows):
                index = i - (i > last).astype(jnp.int32)
                panel[rows, pl.ds(pl.multiple_of(index * snps, snps), snps)] = ref[i]

    order = [len(keys) - 1, *range(len(keys) - 1)]
    for i, t in enumerate(order):
        if i >= 2:
            out_copy(order[i - 2]).wait()
        if i == 0:
            before = lax.dot_general(
                panel[:, : (n - 1) * snps], begun[...], dims, preferred_element_type=jnp.float32
            )
            left = panel[:, (n - 1) * snps :]
        else:
            rows = pl.ds(t * 2 * sub, 2 * sub)
            before, left = early[rows, :], rest[rows, :]
        product = lax.dot_general(left, block[...], dims, preferred_element_type=jnp.float32)
        tile[t % 2] = (before + product) / (n * snps)
        out_copy(t).start()
    for t in order[-2:]:
        out_copy(t).wait()


def limit(arrays):
    return min(sum(math.prod(a.shape) * a.dtype.itemsize for a in arrays) + 4 * 2**20, 60 * 2**20)


def multiply(own, near, got, panels, keys):
    n, sub, snps = near.shape
    rows, cols = (len(panels) - 2) * sub, own.shape[0]
    plan = tuple(key for key in got if key[1] < n - 1)
    width = 256 if cols % 256 == 0 else cols
    scratch = [
        pltpu.VMEM((rows, (n - 1) * snps), jnp.bfloat16),
        pltpu.VMEM((2, rows, width), jnp.float32),
    ]
    operands = [own, near, *[got[key] for key in plan], *panels[:-2]]
    outs = [
        jax.ShapeDtypeStruct((rows, cols), jnp.float32),
        jax.ShapeDtypeStruct((rows, snps), jnp.bfloat16),
        jax.ShapeDtypeStruct((cols, (n - 1) * snps), jnp.bfloat16),
    ]
    early = pl.pallas_call(
        functools.partial(early_kernel, n, plan),
        out_shape=outs,
        in_specs=[HBM] + [VMEM] * (len(operands) - 1),
        out_specs=[ANY, VMEM, VMEM],
        scratch_shapes=scratch + [pltpu.SemaphoreType.DMA, pltpu.SemaphoreType.DMA((2,))],
        compiler_params=pltpu.CompilerParams(vmem_limit_bytes=limit([*operands[1:], *scratch, *outs[1:]])),
        cost_estimate=pl.CostEstimate(flops=EARLY, bytes_accessed=0, transcendentals=0),
        name="early",
    )(*operands)
    plan = tuple(key for key in got if key[1] >= n // 2)
    operands = [after(near, early[1]), *[got[key] for key in plan]]
    block = pl.pallas_call(
        functools.partial(last_block_kernel, n, plan),
        out_shape=jax.ShapeDtypeStruct((cols, snps), jnp.bfloat16),
        compiler_params=pltpu.CompilerParams(vmem_limit_bytes=limit(operands)),
        cost_estimate=pl.CostEstimate(flops=PACE, bytes_accessed=0, transcendentals=0),
        name="last_block",
    )(*operands)
    operands = [block, *early, *panels[-2:]]
    scratch = [
        pltpu.VMEM((2 * sub, n * snps), jnp.bfloat16),
        pltpu.VMEM((2, 2 * sub, cols), jnp.float32),
    ]
    return pl.pallas_call(
        functools.partial(late_kernel, n, keys),
        out_shape=jax.ShapeDtypeStruct((len(panels) * sub, cols), jnp.float32),
        in_specs=[VMEM] * len(operands),
        out_specs=ANY,
        scratch_shapes=scratch + [pltpu.SemaphoreType.DMA((2,))],
        compiler_params=pltpu.CompilerParams(vmem_limit_bytes=limit([*operands, *scratch])),
        name="late",
    )(*operands)


def after(value, *earlier):
    return lax.optimization_barrier((value, *earlier))[0]


def flip(value, masks):
    size = lax.axis_size("wide")
    return lax.ppermute(value, "wide", [(i, i ^ masks[i & 1]) for i in range(size)])


def spread(panel, earlier):
    size = lax.axis_size("wide")
    bits = [1 << b for b in range(1, size.bit_length() - 1)]
    got = {(0, 0): panel}
    for i in range(len(bits)):
        masks = (bits[i], bits[-1 - i])
        for key, value in list(got.items()):
            if any(key):
                value = after(value, *earlier)
            got[key[0] ^ masks[0], key[1] ^ masks[1]] = flip(value, masks)
    return got


def shards(dosages, allele_counts, called_counts):
    n, wide = lax.axis_size("narrow"), lax.axis_size("wide")
    z, w = lax.axis_index("narrow"), lax.axis_index("wide")
    snps, cols = dosages.shape
    sub = cols // n
    own, panels = standardize(dosages, allele_counts, called_counts, n)
    got = {(swapped, 1): trade(own, swapped, 1) for swapped in range(2)}
    mine = pick(own, sub)
    pieces = [far_swap(after(value, mine), m) for m, value in enumerate(panels, 2)]
    near = stack(mine, got[0, 1], got[1, 1], pieces)
    ready = []
    for step in range(2, n):
        values = hand_on(got[0, step - 1], got[1, step - 1], near, step - 1)
        ready = values if step == min(3, n - 1) else ready
        for swapped, value in enumerate(values):
            got[swapped, step] = trade(value, swapped, step)
    held = spread(near, ready)
    partner = {key: flip(value, (1, 1)) for key, value in held.items()}
    keys = tuple(held)
    panels = [array for key in keys for array in (held[key], partner[key[::-1]])]
    result = multiply(own, near, got, panels, keys)
    return result.reshape(wide, 1, sub, cols)


def solution(mesh):
    return jax.shard_map(
        shards,
        mesh=mesh,
        in_specs=(P("narrow", "wide"), P("narrow"), P("narrow")),
        out_specs=P(None, "narrow", None, "wide"),
        check_vma=False,
    )
```

```python
import functools
import math

import jax
import jax.numpy as jnp
from jax import lax
from jax.experimental import pallas as pl
from jax.experimental.pallas import tpu as pltpu
from jax.sharding import PartitionSpec as P

LANES = 128
HOP = 20_000_000_000
PACE = 10_000_000_000
EARLY = 12_000_000_000
ANY = pl.BlockSpec(memory_space=pl.ANY)
VMEM = pl.BlockSpec(memory_space=pltpu.VMEM)
HBM = pl.BlockSpec(memory_space=pltpu.HBM)


def trade(value, swapped, step):
    n, wide = lax.axis_size("narrow"), lax.axis_size("wide")
    pairs = []
    for w in range(wide):
        for low in range((w + swapped) % 2, n - 1, 2):
            if low + 1 >= step or low + step <= n - 1:
                pairs += [(w * n + low, w * n + low + 1), (w * n + low + 1, w * n + low)]
    return lax.ppermute(value, ("wide", "narrow"), pairs)


def side_of(swapped):
    return lax.rem(lax.axis_index("wide") + swapped, 2)


def partner_on(z, odd):
    side = lax.rem(z + odd, 2)
    return z + 1 - 2 * side


def far_swap(value, mask):
    pairs = [(i, i ^ mask) for i in range(lax.axis_size("narrow"))]
    return lax.ppermute(value, "narrow", [(i, j) for i, j in pairs if abs(i - j) > 1])


def slab_of(z, odd, step):
    side = lax.rem(z + odd, 2)
    return z + step * (1 - 2 * side)


def standardize_kernel(n, dosages_ref, allele_ref, called_ref, own, *refs):
    panels, (dosages, allele, called, sem) = refs[: n - 2], refs[n - 2 :]
    z = lax.axis_index("narrow")
    snps, cols = dosages.shape
    sub = cols // n
    counts = [
        pltpu.make_async_copy(allele_ref, allele, sem.at[0]),
        pltpu.make_async_copy(called_ref, called, sem.at[1]),
    ]
    starts = range(0, snps, LANES)
    doses = [
        pltpu.make_async_copy(dosages_ref.at[pl.ds(start, LANES), :], dosages.at[pl.ds(start, LANES), :], sem.at[2 + i])
        for i, start in enumerate(starts)
    ]
    for copy in counts + doses:
        copy.start()
    for copy in counts:
        copy.wait()

    for i, start in enumerate(starts):
        doses[i].wait()
        lanes = pl.ds(start, LANES)
        freq = allele[:, lanes].astype(jnp.float32) / (2.0 * called[:, lanes].astype(jnp.float32))
        scale = lax.rsqrt(2.0 * freq * (1.0 - freq))
        dose = dosages[lanes, :].astype(jnp.float32).T
        values = jnp.where(dose == 3.0, 0.0, (dose - 2.0 * freq) * scale).astype(jnp.bfloat16)
        own[:, lanes] = values
    for m, ref in enumerate(panels, 2):
        ref[...] = own[pl.ds(pl.multiple_of((z ^ m) * sub, sub), sub), :]


def standardize(dosages, allele_counts, called_counts, n):
    snps, cols = dosages.shape
    sub = cols // n
    shapes = [(cols, snps)] + [(sub, snps)] * (n - 2)
    outs = pl.pallas_call(
        functools.partial(standardize_kernel, n),
        out_shape=[jax.ShapeDtypeStruct(shape, jnp.bfloat16) for shape in shapes],
        in_specs=[pl.BlockSpec(memory_space=pltpu.HBM)] * 3,
        scratch_shapes=[
            pltpu.VMEM((snps, cols), jnp.int32),
            pltpu.VMEM((1, snps), jnp.int32),
            pltpu.VMEM((1, snps), jnp.int32),
            pltpu.SemaphoreType.DMA((2 + snps // LANES,)),
        ],
        compiler_params=pltpu.CompilerParams(vmem_limit_bytes=60 * 2**20),
        name="standardize",
    )(dosages, allele_counts[None], called_counts[None])
    return outs[0], outs[1:]


def pick_kernel(own, out, sem):
    sub = out.shape[0]
    rows = pl.ds(pl.multiple_of(lax.axis_index("narrow") * sub, sub), sub)
    copy = pltpu.make_async_copy(own.at[rows, :], out, sem)
    copy.start()
    copy.wait()


def pick(own, sub):
    return pl.pallas_call(
        pick_kernel,
        out_shape=jax.ShapeDtypeStruct((sub, own.shape[1]), own.dtype),
        in_specs=[ANY],
        out_specs=VMEM,
        scratch_shapes=[pltpu.SemaphoreType.DMA],
        compiler_params=pltpu.CompilerParams(vmem_limit_bytes=2**20),
        name="pick",
    )(own)


def stack_kernel(n, mine, first, second, *refs):
    pieces, out, sem = refs[: n - 2], refs[n - 2], refs[n - 1]
    z = lax.axis_index("narrow")
    sub = out.shape[1]
    rows = pl.ds(pl.multiple_of(z * sub, sub), sub)

    def hops(act):
        for swapped, value in enumerate((first, second)):
            other = partner_on(z, side_of(swapped))

            @pl.when((other >= 0) & (other < n))
            def _(swapped=swapped, value=value, other=other):
                act(pltpu.make_async_copy(value.at[rows, :], out.at[other], sem.at[swapped]))

    hops(lambda copy: copy.start())
    out[z] = mine[...]
    for m, piece in enumerate(pieces, 2):

        @pl.when(jnp.abs((z ^ m) - z) > 1)
        def _(m=m, piece=piece):
            out[z ^ m] = piece[...]

    hops(lambda copy: copy.wait())


def stack(mine, first, second, pieces):
    n = len(pieces) + 2
    return pl.pallas_call(
        functools.partial(stack_kernel, n),
        out_shape=jax.ShapeDtypeStruct((n, *mine.shape), mine.dtype),
        in_specs=[VMEM, ANY, ANY] + [VMEM] * (n - 2),
        out_specs=VMEM,
        scratch_shapes=[pltpu.SemaphoreType.DMA((2,))],
        compiler_params=pltpu.CompilerParams(vmem_limit_bytes=10 * 2**20),
        name="stack",
    )(mine, first, second, *pieces)


def hand_on_kernel(n, step, first, second, near, *outs):
    z, sub = lax.axis_index("narrow"), near.shape[1]
    for swapped, value, out in ((1, second, outs[0]), (0, first, outs[1])):
        odd = side_of(swapped)
        to = jnp.clip(partner_on(z, 1 - odd), 0, n - 1)
        if step == 1:
            for slot in range(n - 1):
                q = slot + (slot >= to).astype(jnp.int32)
                out[pl.ds(slot * sub, sub), :] = value[pl.ds(pl.multiple_of(q * sub, sub), sub), :]
        else:
            out[...] = value[...]
            slab = jnp.clip(slab_of(z, odd, step), 0, n - 1)
            slot = jnp.minimum(jnp.minimum(z, to), n - 2)
            out[pl.ds(pl.multiple_of(slot * sub, sub), sub), :] = near[slab]


def hand_on(first, second, near, step):
    n, sub, snps = near.shape
    return pl.pallas_call(
        functools.partial(hand_on_kernel, n, step),
        out_shape=[jax.ShapeDtypeStruct(((n - 1) * sub, snps), first.dtype)] * 2,
        compiler_params=pltpu.CompilerParams(vmem_limit_bytes=12 * 2**20),
        cost_estimate=pl.CostEstimate(flops=HOP, bytes_accessed=0, transcendentals=0),
        name="hand_on",
    )(first, second, near)


def last_slab(z, n):
    return jnp.where(z < n // 2, n - 1, 0)


def block_copies(n, plan, near, trades, z, go):
    sub = near.shape[1]
    for i in range(n):
        go(near.at[i], z, i)
    for ref, (swapped, step) in zip(trades, plan):
        slab, other = slab_of(z, side_of(swapped), step), partner_on(z, side_of(swapped))

        @pl.when((slab >= 0) & (slab < n) & (other >= 0) & (other < n))
        def _(ref=ref, slab=slab, step=step):
            if step == 1:
                for q in range(n):
                    pl.when(q != z)(lambda q=q: go(ref.at[pl.ds(q * sub, sub), :], q, slab))
            else:
                for slot in range(n - 1):
                    go(ref.at[pl.ds(slot * sub, sub), :], slot + (slot >= z).astype(jnp.int32), slab)


def panel_rows(m, w, sub):
    return pl.ds(pl.multiple_of((m // 2 * 2 + (w + m) % 2) * sub, sub), sub)


def early_kernel(n, plan, own, near, *refs):
    trades, (*panels, out, rest, block, panel, tile, own_sem, out_sem) = refs[: len(plan)], refs[len(plan) :]
    z, w = lax.axis_index("narrow"), lax.axis_index("wide")
    cols, snps = own.shape
    sub = cols // n
    last = last_slab(z, n)

    def place(slab):
        index = slab - (slab > last).astype(jnp.int32)
        return pl.ds(pl.multiple_of(index * snps, snps), snps)

    def go(src, q, slab):
        @pl.when(slab != last)
        def _():
            block[pl.ds(pl.multiple_of(q * sub, sub), sub), place(slab)] = src[...]

    def own_copies(act):
        for q in range(n):
            rows = pl.ds(q * sub, sub)

            @pl.when(q != z)
            def _(rows=rows):
                act(pltpu.make_async_copy(own.at[rows, :], block.at[rows, place(z)], own_sem))

    own_copies(lambda copy: copy.start())
    block_copies(n, plan, near, trades, z, go)
    for m, ref in enumerate(panels):
        rows = panel_rows(m, w, sub)
        rest[rows, :] = ref[last]
        for i in range(n):

            @pl.when(i != last)
            def _(i=i, ref=ref, rows=rows):
                panel[rows, place(i)] = ref[i]

    own_copies(lambda copy: copy.wait())
    width = tile.shape[2]
    outs = [
        pltpu.make_async_copy(tile.at[i % 2], out.at[:, pl.ds(start, width)], out_sem.at[i % 2])
        for i, start in enumerate(range(0, cols, width))
    ]
    for i, copy in enumerate(outs):
        if i >= 2:
            outs[i - 2].wait()
        tile[i % 2] = lax.dot_general(
            panel[...], block[pl.ds(i * width, width), :], (((1,), (1,)), ((), ())), preferred_element_type=jnp.float32
        )
        copy.start()
    for copy in outs[-2:]:
        copy.wait()


def last_block_kernel(n, plan, near, *refs):
    trades, block = refs[:-1], refs[-1]
    z, sub = lax.axis_index("narrow"), near.shape[1]
    last = last_slab(z, n)

    def go(src, q, slab):
        @pl.when(slab == last)
        def _():
            block[pl.ds(pl.multiple_of(q * sub, sub), sub), :] = src[...]

    block_copies(n, plan, near, trades, z, go)


def late_kernel(n, keys, block, early, rest, begun, *refs):
    halves, (out, panel, tile, out_sem) = refs[:4], refs[4:]
    z, w = lax.axis_index("narrow"), lax.axis_index("wide")
    cols, snps = block.shape
    sub = cols // n
    last = last_slab(z, n)
    dims = (((1,), (1,)), ((), ()))

    def out_copy(t):
        chip = (w ^ jnp.where(lax.rem(w, 2) == 0, *keys[t])) // 2
        rows = pl.ds(pl.multiple_of(chip * (2 * sub), 2 * sub), 2 * sub)
        return pltpu.make_async_copy(tile.at[t % 2], out.at[rows], out_sem.at[t % 2])

    for m in range(2):
        rows = panel_rows(m, w, sub)
        for i in range(n):
            index = jnp.where(i == last, n - 1, i - (i > last).astype(jnp.int32))
            ref = halves[2 * m + i // (n // 2)]
            panel[rows, pl.ds(pl.multiple_of(index * snps, snps), snps)] = ref[i % (n // 2)]

    order = [len(keys) - 1, *range(len(keys) - 1)]
    for i, t in enumerate(order):
        if i >= 2:
            out_copy(order[i - 2]).wait()
        if i == 0:
            before = lax.dot_general(
                panel[:, : (n - 1) * snps], begun[...], dims, preferred_element_type=jnp.float32
            )
            left = panel[:, (n - 1) * snps :]
        else:
            rows = pl.ds(t * 2 * sub, 2 * sub)
            before, left = early[rows, :], rest[rows, :]
        product = lax.dot_general(left, block[...], dims, preferred_element_type=jnp.float32)
        tile[t % 2] = (before + product) / (n * snps)
        out_copy(t).start()
    for t in order[-2:]:
        out_copy(t).wait()


def limit(arrays):
    return min(sum(math.prod(a.shape) * a.dtype.itemsize for a in arrays) + 4 * 2**20, 60 * 2**20)


def multiply(own, near, got, panels, halves, keys):
    n, sub, snps = near.shape
    rows, cols = len(panels) * sub, own.shape[0]
    plan = tuple(key for key in got if key[1] < n - 1)
    width = 256 if cols % 256 == 0 else cols
    scratch = [
        pltpu.VMEM((rows, (n - 1) * snps), jnp.bfloat16),
        pltpu.VMEM((2, rows, width), jnp.float32),
    ]
    operands = [own, near, *[got[key] for key in plan], *panels]
    outs = [
        jax.ShapeDtypeStruct((rows, cols), jnp.float32),
        jax.ShapeDtypeStruct((rows, snps), jnp.bfloat16),
        jax.ShapeDtypeStruct((cols, (n - 1) * snps), jnp.bfloat16),
    ]
    early = pl.pallas_call(
        functools.partial(early_kernel, n, plan),
        out_shape=outs,
        in_specs=[HBM] + [VMEM] * (len(operands) - 1),
        out_specs=[ANY, VMEM, VMEM],
        scratch_shapes=scratch + [pltpu.SemaphoreType.DMA, pltpu.SemaphoreType.DMA((2,))],
        compiler_params=pltpu.CompilerParams(vmem_limit_bytes=limit([*operands[1:], *scratch, *outs[1:]])),
        cost_estimate=pl.CostEstimate(flops=EARLY, bytes_accessed=0, transcendentals=0),
        name="early",
    )(*operands)
    plan = tuple(key for key in got if key[1] >= n // 2)
    operands = [after(near, early[1]), *[got[key] for key in plan]]
    block = pl.pallas_call(
        functools.partial(last_block_kernel, n, plan),
        out_shape=jax.ShapeDtypeStruct((cols, snps), jnp.bfloat16),
        compiler_params=pltpu.CompilerParams(vmem_limit_bytes=limit(operands)),
        cost_estimate=pl.CostEstimate(flops=PACE, bytes_accessed=0, transcendentals=0),
        name="last_block",
    )(*operands)
    operands = [block, *early, *halves, *[flip(after(half, early[1]), (1, 1)) for half in halves]]
    scratch = [
        pltpu.VMEM((2 * sub, n * snps), jnp.bfloat16),
        pltpu.VMEM((2, 2 * sub, cols), jnp.float32),
    ]
    return pl.pallas_call(
        functools.partial(late_kernel, n, keys),
        out_shape=jax.ShapeDtypeStruct((rows + 2 * sub, cols), jnp.float32),
        in_specs=[VMEM] * len(operands),
        out_specs=ANY,
        scratch_shapes=scratch + [pltpu.SemaphoreType.DMA((2,))],
        compiler_params=pltpu.CompilerParams(vmem_limit_bytes=limit([*operands, *scratch])),
        name="late",
    )(*operands)


def after(value, *earlier):
    return lax.optimization_barrier((value, *earlier))[0]


def flip(value, masks):
    size = lax.axis_size("wide")
    return lax.ppermute(value, "wide", [(i, i ^ masks[i & 1]) for i in range(size)])


def spread(panel, earlier):
    size = lax.axis_size("wide")
    bits = [1 << b for b in range(1, size.bit_length() - 1)]
    got = {(0, 0): panel}
    for i in range(len(bits)):
        masks = (bits[i], bits[-1 - i])
        for key, value in list(got.items()):
            if any(key):
                value = after(value, *earlier)
            to = key[0] ^ masks[0], key[1] ^ masks[1]
            if to == (size - 2, size - 2):
                half = value.shape[0] // 2
                got[to] = [flip(value[:half], masks), flip(value[half:], masks)]
            else:
                got[to] = flip(value, masks)
    return got


def shards(dosages, allele_counts, called_counts):
    n, wide = lax.axis_size("narrow"), lax.axis_size("wide")
    z, w = lax.axis_index("narrow"), lax.axis_index("wide")
    snps, cols = dosages.shape
    sub = cols // n
    own, panels = standardize(dosages, allele_counts, called_counts, n)
    got = {(swapped, 1): trade(own, swapped, 1) for swapped in range(2)}
    mine = pick(own, sub)
    pieces = [far_swap(after(value, mine), m) for m, value in enumerate(panels, 2)]
    near = stack(mine, got[0, 1], got[1, 1], pieces)
    ready = []
    for step in range(2, n):
        values = hand_on(got[0, step - 1], got[1, step - 1], near, step - 1)
        ready = values if step == min(3, n - 1) else ready
        for swapped, value in enumerate(values):
            got[swapped, step] = trade(value, swapped, step)
    held = spread(near, ready)
    *keys, final = held
    partner = {key: flip(held[key], (1, 1)) for key in keys}
    panels = [array for key in keys for array in (held[key], partner[key[::-1]])]
    result = multiply(own, near, got, panels, held[final], tuple(held))
    return result.reshape(wide, 1, sub, cols)


def solution(mesh):
    return jax.shard_map(
        shards,
        mesh=mesh,
        in_specs=(P("narrow", "wide"), P("narrow"), P("narrow")),
        out_specs=P(None, "narrow", None, "wide"),
        check_vma=False,
    )
```

```python
import functools
import math

import jax
import jax.numpy as jnp
from jax import lax
from jax.experimental import pallas as pl
from jax.experimental.pallas import tpu as pltpu
from jax.sharding import PartitionSpec as P

LANES = 128
HOP = 20_000_000_000
MIDDLE = 0
EARLY = 12_000_000_000
ANY = pl.BlockSpec(memory_space=pl.ANY)
VMEM = pl.BlockSpec(memory_space=pltpu.VMEM)
HBM = pl.BlockSpec(memory_space=pltpu.HBM)


def trade(value, swapped, step):
    n, wide = lax.axis_size("narrow"), lax.axis_size("wide")
    pairs = []
    for w in range(wide):
        for low in range((w + swapped) % 2, n - 1, 2):
            if low + 1 >= step or low + step <= n - 1:
                pairs += [(w * n + low, w * n + low + 1), (w * n + low + 1, w * n + low)]
    return lax.ppermute(value, ("wide", "narrow"), pairs)


def side_of(swapped):
    return lax.rem(lax.axis_index("wide") + swapped, 2)


def partner_on(z, odd):
    side = lax.rem(z + odd, 2)
    return z + 1 - 2 * side


def far_swap(value, mask):
    pairs = [(i, i ^ mask) for i in range(lax.axis_size("narrow"))]
    return lax.ppermute(value, "narrow", [(i, j) for i, j in pairs if abs(i - j) > 1])


def slab_of(z, odd, step):
    side = lax.rem(z + odd, 2)
    return z + step * (1 - 2 * side)


def standardize_kernel(n, dosages_ref, allele_ref, called_ref, own, *refs):
    panels, (dosages, allele, called, sem) = refs[: n - 2], refs[n - 2 :]
    z = lax.axis_index("narrow")
    snps, cols = dosages.shape
    sub = cols // n
    counts = [
        pltpu.make_async_copy(allele_ref, allele, sem.at[0]),
        pltpu.make_async_copy(called_ref, called, sem.at[1]),
    ]
    starts = range(0, snps, LANES)
    doses = [
        pltpu.make_async_copy(dosages_ref.at[pl.ds(start, LANES), :], dosages.at[pl.ds(start, LANES), :], sem.at[2 + i])
        for i, start in enumerate(starts)
    ]
    for copy in counts + doses:
        copy.start()
    for copy in counts:
        copy.wait()

    for i, start in enumerate(starts):
        doses[i].wait()
        lanes = pl.ds(start, LANES)
        freq = allele[:, lanes].astype(jnp.float32) / (2.0 * called[:, lanes].astype(jnp.float32))
        scale = lax.rsqrt(2.0 * freq * (1.0 - freq))
        dose = dosages[lanes, :].astype(jnp.float32).T
        values = jnp.where(dose == 3.0, 0.0, (dose - 2.0 * freq) * scale).astype(jnp.bfloat16)
        own[:, lanes] = values
    for m, ref in enumerate(panels, 2):
        ref[...] = own[pl.ds(pl.multiple_of((z ^ m) * sub, sub), sub), :]


def standardize(dosages, allele_counts, called_counts, n):
    snps, cols = dosages.shape
    sub = cols // n
    shapes = [(cols, snps)] + [(sub, snps)] * (n - 2)
    outs = pl.pallas_call(
        functools.partial(standardize_kernel, n),
        out_shape=[jax.ShapeDtypeStruct(shape, jnp.bfloat16) for shape in shapes],
        in_specs=[pl.BlockSpec(memory_space=pltpu.HBM)] * 3,
        scratch_shapes=[
            pltpu.VMEM((snps, cols), jnp.int32),
            pltpu.VMEM((1, snps), jnp.int32),
            pltpu.VMEM((1, snps), jnp.int32),
            pltpu.SemaphoreType.DMA((2 + snps // LANES,)),
        ],
        compiler_params=pltpu.CompilerParams(vmem_limit_bytes=60 * 2**20),
        name="standardize",
    )(dosages, allele_counts[None], called_counts[None])
    return outs[0], outs[1:]


def pick_kernel(own, out, sem):
    sub = out.shape[0]
    rows = pl.ds(pl.multiple_of(lax.axis_index("narrow") * sub, sub), sub)
    copy = pltpu.make_async_copy(own.at[rows, :], out, sem)
    copy.start()
    copy.wait()


def pick(own, sub):
    return pl.pallas_call(
        pick_kernel,
        out_shape=jax.ShapeDtypeStruct((sub, own.shape[1]), own.dtype),
        in_specs=[ANY],
        out_specs=VMEM,
        scratch_shapes=[pltpu.SemaphoreType.DMA],
        compiler_params=pltpu.CompilerParams(vmem_limit_bytes=2**20),
        name="pick",
    )(own)


def stack_kernel(n, mine, first, second, *refs):
    pieces, out, sem = refs[: n - 2], refs[n - 2], refs[n - 1]
    z = lax.axis_index("narrow")
    sub = out.shape[1]
    rows = pl.ds(pl.multiple_of(z * sub, sub), sub)

    def hops(act):
        for swapped, value in enumerate((first, second)):
            other = partner_on(z, side_of(swapped))

            @pl.when((other >= 0) & (other < n))
            def _(swapped=swapped, value=value, other=other):
                act(pltpu.make_async_copy(value.at[rows, :], out.at[other], sem.at[swapped]))

    hops(lambda copy: copy.start())
    out[z] = mine[...]
    for m, piece in enumerate(pieces, 2):

        @pl.when(jnp.abs((z ^ m) - z) > 1)
        def _(m=m, piece=piece):
            out[z ^ m] = piece[...]

    hops(lambda copy: copy.wait())


def stack(mine, first, second, pieces):
    n = len(pieces) + 2
    return pl.pallas_call(
        functools.partial(stack_kernel, n),
        out_shape=jax.ShapeDtypeStruct((n, *mine.shape), mine.dtype),
        in_specs=[VMEM, ANY, ANY] + [VMEM] * (n - 2),
        out_specs=VMEM,
        scratch_shapes=[pltpu.SemaphoreType.DMA((2,))],
        compiler_params=pltpu.CompilerParams(vmem_limit_bytes=10 * 2**20),
        name="stack",
    )(mine, first, second, *pieces)


def hand_on_kernel(n, step, first, second, near, *outs):
    z, sub = lax.axis_index("narrow"), near.shape[1]
    for swapped, value, out in ((1, second, outs[0]), (0, first, outs[1])):
        odd = side_of(swapped)
        to = jnp.clip(partner_on(z, 1 - odd), 0, n - 1)
        if step == 1:
            for slot in range(n - 1):
                q = slot + (slot >= to).astype(jnp.int32)
                out[pl.ds(slot * sub, sub), :] = value[pl.ds(pl.multiple_of(q * sub, sub), sub), :]
        else:
            out[...] = value[...]
            slab = jnp.clip(slab_of(z, odd, step), 0, n - 1)
            slot = jnp.minimum(jnp.minimum(z, to), n - 2)
            out[pl.ds(pl.multiple_of(slot * sub, sub), sub), :] = near[slab]


def hand_on(first, second, near, step):
    n, sub, snps = near.shape
    return pl.pallas_call(
        functools.partial(hand_on_kernel, n, step),
        out_shape=[jax.ShapeDtypeStruct(((n - 1) * sub, snps), first.dtype)] * 2,
        compiler_params=pltpu.CompilerParams(vmem_limit_bytes=12 * 2**20),
        cost_estimate=pl.CostEstimate(flops=HOP, bytes_accessed=0, transcendentals=0),
        name="hand_on",
    )(first, second, near)


def last_slab(z, n):
    return jnp.where(z < n // 2, n - 1, 0)


def block_copies(n, plan, near, trades, z, go):
    sub = near.shape[1]
    for i in range(n):
        go(near.at[i], z, i)
    for ref, (swapped, step) in zip(trades, plan):
        slab, other = slab_of(z, side_of(swapped), step), partner_on(z, side_of(swapped))

        @pl.when((slab >= 0) & (slab < n) & (other >= 0) & (other < n))
        def _(ref=ref, slab=slab, step=step):
            if step == 1:
                for q in range(n):
                    pl.when(q != z)(lambda q=q: go(ref.at[pl.ds(q * sub, sub), :], q, slab))
            else:
                for slot in range(n - 1):
                    go(ref.at[pl.ds(slot * sub, sub), :], slot + (slot >= z).astype(jnp.int32), slab)


def panel_rows(m, w, sub):
    return pl.ds(pl.multiple_of((m // 2 * 2 + (w + m) % 2) * sub, sub), sub)


def early_kernel(n, plan, own, near, *refs):
    trades, (*panels, out, rest, block, panel, tile, own_sem, out_sem) = refs[: len(plan)], refs[len(plan) :]
    z, w = lax.axis_index("narrow"), lax.axis_index("wide")
    cols, snps = own.shape
    sub = cols // n
    last = last_slab(z, n)

    def place(slab):
        index = slab - (slab > last).astype(jnp.int32)
        return pl.ds(pl.multiple_of(index * snps, snps), snps)

    def go(src, q, slab):
        @pl.when(slab != last)
        def _():
            block[pl.ds(pl.multiple_of(q * sub, sub), sub), place(slab)] = src[...]

    def own_copies(act):
        for q in range(n):
            rows = pl.ds(q * sub, sub)

            @pl.when(q != z)
            def _(rows=rows):
                act(pltpu.make_async_copy(own.at[rows, :], block.at[rows, place(z)], own_sem))

    own_copies(lambda copy: copy.start())
    block_copies(n, plan, near, trades, z, go)
    for m, ref in enumerate(panels):
        rows = panel_rows(m, w, sub)
        rest[rows, :] = ref[last]
        for i in range(n):

            @pl.when(i != last)
            def _(i=i, ref=ref, rows=rows):
                panel[rows, place(i)] = ref[i]

    own_copies(lambda copy: copy.wait())
    width = tile.shape[2]
    outs = [
        pltpu.make_async_copy(tile.at[i % 2], out.at[:, pl.ds(start, width)], out_sem.at[i % 2])
        for i, start in enumerate(range(0, cols, width))
    ]
    for i, copy in enumerate(outs):
        if i >= 2:
            outs[i - 2].wait()
        tile[i % 2] = lax.dot_general(
            panel[...], block[pl.ds(i * width, width), :], (((1,), (1,)), ((), ())), preferred_element_type=jnp.float32
        )
        copy.start()
    for copy in outs[-2:]:
        copy.wait()


def last_block_kernel(n, plan, near, *refs):
    trades, block = refs[:-1], refs[-1]
    z, sub = lax.axis_index("narrow"), near.shape[1]
    last = last_slab(z, n)

    def go(src, q, slab):
        @pl.when(slab == last)
        def _():
            block[pl.ds(pl.multiple_of(q * sub, sub), sub), :] = src[...]

    block_copies(n, plan, near, trades, z, go)


def middle_kernel(n, begun, *refs):
    halves, (out, rest, panel) = refs[:4], refs[4:]
    w, last = lax.axis_index("wide"), last_slab(lax.axis_index("narrow"), n)
    _, sub, snps = halves[0].shape
    for m in range(2):
        rows = panel_rows(m, w, sub)
        for i in range(n):
            ref = halves[2 * m + i // (n // 2)]

            @pl.when(i == last)
            def _(i=i, ref=ref, rows=rows):
                rest[rows, :] = ref[i % (n // 2)]

            @pl.when(i != last)
            def _(i=i, ref=ref, rows=rows):
                index = i - (i > last).astype(jnp.int32)
                panel[rows, pl.ds(pl.multiple_of(index * snps, snps), snps)] = ref[i % (n // 2)]

    out[...] = lax.dot_general(panel[...], begun[...], (((1,), (1,)), ((), ())), preferred_element_type=jnp.float32)


def late_kernel(n, keys, block, early, early_rest, middle, middle_rest, out, tile, out_sem):
    w = lax.axis_index("wide")
    snps, size = block.shape[1], middle.shape[0]
    slots = tile.shape[0]

    def out_copy(t):
        chip = (w ^ jnp.where(lax.rem(w, 2) == 0, *keys[t])) // 2
        rows = pl.ds(pl.multiple_of(chip * size, size), size)
        return pltpu.make_async_copy(tile.at[t % slots], out.at[rows], out_sem.at[t % slots])

    for t in range(len(keys)):
        if t >= slots:
            out_copy(t - slots).wait()
        if t < len(keys) - 1:
            rows = pl.ds(t * size, size)
            before, left = early[rows, :], early_rest[rows, :]
        else:
            before, left = middle[...], middle_rest[...]
        product = lax.dot_general(left, block[...], (((1,), (1,)), ((), ())), preferred_element_type=jnp.float32)
        tile[t % slots] = (before + product) / (n * snps)
        out_copy(t).start()
    for t in range(max(len(keys) - slots, 0), len(keys)):
        out_copy(t).wait()


def limit(arrays):
    return min(sum(math.prod(a.shape) * a.dtype.itemsize for a in arrays) + 4 * 2**20, 60 * 2**20)


def multiply(own, near, got, panels, halves, keys):
    n, sub, snps = near.shape
    rows, cols = len(panels) * sub, own.shape[0]
    plan = tuple(key for key in got if key[1] < n - 1)
    width = 256 if cols % 256 == 0 else cols
    scratch = [
        pltpu.VMEM((rows, (n - 1) * snps), jnp.bfloat16),
        pltpu.VMEM((2, rows, width), jnp.float32),
    ]
    operands = [own, near, *[got[key] for key in plan], *panels]
    outs = [
        jax.ShapeDtypeStruct((rows, cols), jnp.float32),
        jax.ShapeDtypeStruct((rows, snps), jnp.bfloat16),
        jax.ShapeDtypeStruct((cols, (n - 1) * snps), jnp.bfloat16),
    ]
    early = pl.pallas_call(
        functools.partial(early_kernel, n, plan),
        out_shape=outs,
        in_specs=[HBM] + [VMEM] * (len(operands) - 1),
        out_specs=[ANY, VMEM, VMEM],
        scratch_shapes=scratch + [pltpu.SemaphoreType.DMA, pltpu.SemaphoreType.DMA((2,))],
        compiler_params=pltpu.CompilerParams(vmem_limit_bytes=limit([*operands[1:], *scratch, *outs[1:]])),
        cost_estimate=pl.CostEstimate(flops=EARLY, bytes_accessed=0, transcendentals=0),
        name="early",
    )(*operands)
    plan = tuple(key for key in got if key[1] >= n // 2)
    operands = [early[2], *halves, *[flip(after(half, early[1]), (1, 1)) for half in halves]]
    outs = [
        jax.ShapeDtypeStruct((2 * sub, cols), jnp.float32),
        jax.ShapeDtypeStruct((2 * sub, snps), jnp.bfloat16),
    ]
    scratch = [pltpu.VMEM((2 * sub, (n - 1) * snps), jnp.bfloat16)]
    middle = pl.pallas_call(
        functools.partial(middle_kernel, n),
        out_shape=outs,
        scratch_shapes=scratch,
        compiler_params=pltpu.CompilerParams(vmem_limit_bytes=limit([*operands, *scratch, *outs])),
        cost_estimate=pl.CostEstimate(flops=MIDDLE, bytes_accessed=0, transcendentals=0),
        name="middle",
    )(*operands)
    operands = [after(near, middle[1]), *[got[key] for key in plan]]
    block = pl.pallas_call(
        functools.partial(last_block_kernel, n, plan),
        out_shape=jax.ShapeDtypeStruct((cols, snps), jnp.bfloat16),
        compiler_params=pltpu.CompilerParams(vmem_limit_bytes=limit(operands)),
        name="last_block",
    )(*operands)
    operands = [block, *early[:2], *middle]
    slots = min(4, len(keys))
    scratch = [pltpu.VMEM((slots, 2 * sub, cols), jnp.float32)]
    return pl.pallas_call(
        functools.partial(late_kernel, n, keys),
        out_shape=jax.ShapeDtypeStruct((rows + 2 * sub, cols), jnp.float32),
        in_specs=[VMEM] * len(operands),
        out_specs=ANY,
        scratch_shapes=scratch + [pltpu.SemaphoreType.DMA((slots,))],
        compiler_params=pltpu.CompilerParams(vmem_limit_bytes=limit([*operands, *scratch])),
        name="late",
    )(*operands)


def after(value, *earlier):
    return lax.optimization_barrier((value, *earlier))[0]


def flip(value, masks):
    size = lax.axis_size("wide")
    return lax.ppermute(value, "wide", [(i, i ^ masks[i & 1]) for i in range(size)])


def spread(panel, earlier):
    size = lax.axis_size("wide")
    bits = [1 << b for b in range(1, size.bit_length() - 1)]
    got = {(0, 0): panel}
    for i in range(len(bits)):
        masks = (bits[i], bits[-1 - i])
        for key, value in list(got.items()):
            if any(key):
                value = after(value, *earlier)
            to = key[0] ^ masks[0], key[1] ^ masks[1]
            if to == (size - 2, size - 2):
                half = value.shape[0] // 2
                got[to] = [flip(value[:half], masks), flip(value[half:], masks)]
            else:
                got[to] = flip(value, masks)
    return got


def shards(dosages, allele_counts, called_counts):
    n, wide = lax.axis_size("narrow"), lax.axis_size("wide")
    z, w = lax.axis_index("narrow"), lax.axis_index("wide")
    snps, cols = dosages.shape
    sub = cols // n
    own, panels = standardize(dosages, allele_counts, called_counts, n)
    got = {(swapped, 1): trade(own, swapped, 1) for swapped in range(2)}
    mine = pick(own, sub)
    pieces = [far_swap(after(value, mine), m) for m, value in enumerate(panels, 2)]
    near = stack(mine, got[0, 1], got[1, 1], pieces)
    ready = []
    for step in range(2, n):
        values = hand_on(got[0, step - 1], got[1, step - 1], near, step - 1)
        ready = values if step == min(3, n - 1) else ready
        for swapped, value in enumerate(values):
            got[swapped, step] = trade(value, swapped, step)
    held = spread(near, ready)
    *keys, final = held
    partner = {key: flip(held[key], (1, 1)) for key in keys}
    panels = [array for key in keys for array in (held[key], partner[key[::-1]])]
    result = multiply(own, near, got, panels, held[final], tuple(held))
    return result.reshape(wide, 1, sub, cols)


def solution(mesh):
    return jax.shard_map(
        shards,
        mesh=mesh,
        in_specs=(P("narrow", "wide"), P("narrow"), P("narrow")),
        out_specs=P(None, "narrow", None, "wide"),
        check_vma=False,
    )
```

```python
import functools
import math

import jax
import jax.numpy as jnp
from jax import lax
from jax.experimental import pallas as pl
from jax.experimental.pallas import tpu as pltpu
from jax.sharding import PartitionSpec as P

LANES = 128
HOP = 20_000_000_000
MIDDLE = 0
EARLY = 12_000_000_000
ANY = pl.BlockSpec(memory_space=pl.ANY)
VMEM = pl.BlockSpec(memory_space=pltpu.VMEM)
HBM = pl.BlockSpec(memory_space=pltpu.HBM)


def trade(value, swapped, step):
    n, wide = lax.axis_size("narrow"), lax.axis_size("wide")
    pairs = []
    for w in range(wide):
        for low in range((w + swapped) % 2, n - 1, 2):
            if low + 1 >= step or low + step <= n - 1:
                pairs += [(w * n + low, w * n + low + 1), (w * n + low + 1, w * n + low)]
    return lax.ppermute(value, ("wide", "narrow"), pairs)


def side_of(swapped):
    return lax.rem(lax.axis_index("wide") + swapped, 2)


def partner_on(z, odd):
    side = lax.rem(z + odd, 2)
    return z + 1 - 2 * side


def far_swap(value, mask):
    pairs = [(i, i ^ mask) for i in range(lax.axis_size("narrow"))]
    return lax.ppermute(value, "narrow", [(i, j) for i, j in pairs if abs(i - j) > 1])


def slab_of(z, odd, step):
    side = lax.rem(z + odd, 2)
    return z + step * (1 - 2 * side)


def standardize_kernel(n, dosages_ref, allele_ref, called_ref, own, *refs):
    panels, (dosages, allele, called, block, sem, out_sem) = refs[: n - 2], refs[n - 2 :]
    z = lax.axis_index("narrow")
    snps, cols = dosages.shape
    sub = cols // n
    counts = [
        pltpu.make_async_copy(allele_ref, allele, sem.at[0]),
        pltpu.make_async_copy(called_ref, called, sem.at[1]),
    ]
    starts = range(0, snps, LANES)
    doses = [
        pltpu.make_async_copy(dosages_ref.at[pl.ds(start, LANES), :], dosages.at[pl.ds(start, LANES), :], sem.at[2 + i])
        for i, start in enumerate(starts)
    ]
    for copy in counts + doses:
        copy.start()
    for copy in counts:
        copy.wait()

    outs = []
    for i, start in enumerate(starts):
        doses[i].wait()
        lanes = pl.ds(start, LANES)
        freq = allele[:, lanes].astype(jnp.float32) / (2.0 * called[:, lanes].astype(jnp.float32))
        scale = lax.rsqrt(2.0 * freq * (1.0 - freq))
        dose = dosages[lanes, :].astype(jnp.float32).T
        values = jnp.where(dose == 3.0, 0.0, (dose - 2.0 * freq) * scale).astype(jnp.bfloat16)
        block[:, lanes] = values
        outs.append(pltpu.make_async_copy(block.at[:, lanes], own.at[:, lanes], out_sem.at[i]))
        outs[-1].start()
    for m, ref in enumerate(panels, 2):
        rows = pl.ds(pl.multiple_of((z ^ m) * sub, sub), sub)
        outs.append(pltpu.make_async_copy(block.at[rows, :], ref, out_sem.at[len(outs)]))
        outs[-1].start()
    for copy in outs:
        copy.wait()


def standardize(dosages, allele_counts, called_counts, n):
    snps, cols = dosages.shape
    sub = cols // n
    shapes = [(cols, snps)] + [(sub, snps)] * (n - 2)
    outs = pl.pallas_call(
        functools.partial(standardize_kernel, n),
        out_shape=[jax.ShapeDtypeStruct(shape, jnp.bfloat16) for shape in shapes],
        in_specs=[HBM] * 3,
        out_specs=[ANY] * len(shapes),
        scratch_shapes=[
            pltpu.VMEM((snps, cols), jnp.int32),
            pltpu.VMEM((1, snps), jnp.int32),
            pltpu.VMEM((1, snps), jnp.int32),
            pltpu.VMEM((cols, snps), jnp.bfloat16),
            pltpu.SemaphoreType.DMA((2 + snps // LANES,)),
            pltpu.SemaphoreType.DMA((snps // LANES + n - 2,)),
        ],
        compiler_params=pltpu.CompilerParams(vmem_limit_bytes=60 * 2**20),
        name="standardize",
    )(dosages, allele_counts[None], called_counts[None])
    return outs[0], outs[1:]


def pick_kernel(own, out, sem):
    sub = out.shape[0]
    rows = pl.ds(pl.multiple_of(lax.axis_index("narrow") * sub, sub), sub)
    copy = pltpu.make_async_copy(own.at[rows, :], out, sem)
    copy.start()
    copy.wait()


def pick(own, sub):
    return pl.pallas_call(
        pick_kernel,
        out_shape=jax.ShapeDtypeStruct((sub, own.shape[1]), own.dtype),
        in_specs=[ANY],
        out_specs=VMEM,
        scratch_shapes=[pltpu.SemaphoreType.DMA],
        compiler_params=pltpu.CompilerParams(vmem_limit_bytes=2**20),
        name="pick",
    )(own)


def stack_kernel(n, mine, first, second, *refs):
    pieces, out, sem = refs[: n - 2], refs[n - 2], refs[n - 1]
    z = lax.axis_index("narrow")
    sub = out.shape[1]
    rows = pl.ds(pl.multiple_of(z * sub, sub), sub)

    def hops(act):
        for swapped, value in enumerate((first, second)):
            other = partner_on(z, side_of(swapped))

            @pl.when((other >= 0) & (other < n))
            def _(swapped=swapped, value=value, other=other):
                act(pltpu.make_async_copy(value.at[rows, :], out.at[other], sem.at[swapped]))

    hops(lambda copy: copy.start())
    out[z] = mine[...]
    for m, piece in enumerate(pieces, 2):

        @pl.when(jnp.abs((z ^ m) - z) > 1)
        def _(m=m, piece=piece):
            out[z ^ m] = piece[...]

    hops(lambda copy: copy.wait())


def stack(mine, first, second, pieces):
    n = len(pieces) + 2
    return pl.pallas_call(
        functools.partial(stack_kernel, n),
        out_shape=jax.ShapeDtypeStruct((n, *mine.shape), mine.dtype),
        in_specs=[VMEM, ANY, ANY] + [VMEM] * (n - 2),
        out_specs=VMEM,
        scratch_shapes=[pltpu.SemaphoreType.DMA((2,))],
        compiler_params=pltpu.CompilerParams(vmem_limit_bytes=10 * 2**20),
        name="stack",
    )(mine, first, second, *pieces)


def hand_on_kernel(n, step, first, second, near, *outs):
    z, sub = lax.axis_index("narrow"), near.shape[1]
    for swapped, value, out in ((1, second, outs[0]), (0, first, outs[1])):
        odd = side_of(swapped)
        to = jnp.clip(partner_on(z, 1 - odd), 0, n - 1)
        if step == 1:
            for slot in range(n - 1):
                q = slot + (slot >= to).astype(jnp.int32)
                out[pl.ds(slot * sub, sub), :] = value[pl.ds(pl.multiple_of(q * sub, sub), sub), :]
        else:
            out[...] = value[...]
            slab = jnp.clip(slab_of(z, odd, step), 0, n - 1)
            slot = jnp.minimum(jnp.minimum(z, to), n - 2)
            out[pl.ds(pl.multiple_of(slot * sub, sub), sub), :] = near[slab]


def hand_on(first, second, near, step):
    n, sub, snps = near.shape
    return pl.pallas_call(
        functools.partial(hand_on_kernel, n, step),
        out_shape=[jax.ShapeDtypeStruct(((n - 1) * sub, snps), first.dtype)] * 2,
        compiler_params=pltpu.CompilerParams(vmem_limit_bytes=12 * 2**20),
        cost_estimate=pl.CostEstimate(flops=HOP, bytes_accessed=0, transcendentals=0),
        name="hand_on",
    )(first, second, near)


def last_slab(z, n):
    return jnp.where(z < n // 2, n - 1, 0)


def block_copies(n, plan, near, trades, z, go):
    sub = near.shape[1]
    for i in range(n):
        go(near.at[i], z, i)
    for ref, (swapped, step) in zip(trades, plan):
        slab, other = slab_of(z, side_of(swapped), step), partner_on(z, side_of(swapped))

        @pl.when((slab >= 0) & (slab < n) & (other >= 0) & (other < n))
        def _(ref=ref, slab=slab, step=step):
            if step == 1:
                for q in range(n):
                    pl.when(q != z)(lambda q=q: go(ref.at[pl.ds(q * sub, sub), :], q, slab))
            else:
                for slot in range(n - 1):
                    go(ref.at[pl.ds(slot * sub, sub), :], slot + (slot >= z).astype(jnp.int32), slab)


def panel_rows(m, w, sub):
    return pl.ds(pl.multiple_of((m // 2 * 2 + (w + m) % 2) * sub, sub), sub)


def early_kernel(n, plan, own, near, *refs):
    trades, (*panels, out, rest, block, panel, tile, own_sem, out_sem) = refs[: len(plan)], refs[len(plan) :]
    z, w = lax.axis_index("narrow"), lax.axis_index("wide")
    cols, snps = own.shape
    sub = cols // n
    last = last_slab(z, n)

    def place(slab):
        index = slab - (slab > last).astype(jnp.int32)
        return pl.ds(pl.multiple_of(index * snps, snps), snps)

    def go(src, q, slab):
        @pl.when(slab != last)
        def _():
            block[pl.ds(pl.multiple_of(q * sub, sub), sub), place(slab)] = src[...]

    def own_copies(act):
        for q in range(n):
            rows = pl.ds(q * sub, sub)

            @pl.when(q != z)
            def _(rows=rows):
                act(pltpu.make_async_copy(own.at[rows, :], block.at[rows, place(z)], own_sem))

    own_copies(lambda copy: copy.start())
    block_copies(n, plan, near, trades, z, go)
    for m, ref in enumerate(panels):
        rows = panel_rows(m, w, sub)
        rest[rows, :] = ref[last]
        for i in range(n):

            @pl.when(i != last)
            def _(i=i, ref=ref, rows=rows):
                panel[rows, place(i)] = ref[i]

    own_copies(lambda copy: copy.wait())
    width = tile.shape[2]
    outs = [
        pltpu.make_async_copy(tile.at[i % 2], out.at[:, pl.ds(start, width)], out_sem.at[i % 2])
        for i, start in enumerate(range(0, cols, width))
    ]
    for i, copy in enumerate(outs):
        if i >= 2:
            outs[i - 2].wait()
        tile[i % 2] = lax.dot_general(
            panel[...], block[pl.ds(i * width, width), :], (((1,), (1,)), ((), ())), preferred_element_type=jnp.float32
        )
        copy.start()
    for copy in outs[-2:]:
        copy.wait()


def last_block_kernel(n, plan, near, *refs):
    trades, block = refs[:-1], refs[-1]
    z, sub = lax.axis_index("narrow"), near.shape[1]
    last = last_slab(z, n)

    def go(src, q, slab):
        @pl.when(slab == last)
        def _():
            block[pl.ds(pl.multiple_of(q * sub, sub), sub), :] = src[...]

    block_copies(n, plan, near, trades, z, go)


def middle_kernel(n, begun, *refs):
    halves, (out, rest, panel) = refs[:4], refs[4:]
    w, last = lax.axis_index("wide"), last_slab(lax.axis_index("narrow"), n)
    _, sub, snps = halves[0].shape
    for m in range(2):
        rows = panel_rows(m, w, sub)
        for i in range(n):
            ref = halves[2 * m + i // (n // 2)]

            @pl.when(i == last)
            def _(i=i, ref=ref, rows=rows):
                rest[rows, :] = ref[i % (n // 2)]

            @pl.when(i != last)
            def _(i=i, ref=ref, rows=rows):
                index = i - (i > last).astype(jnp.int32)
                panel[rows, pl.ds(pl.multiple_of(index * snps, snps), snps)] = ref[i % (n // 2)]

    out[...] = lax.dot_general(panel[...], begun[...], (((1,), (1,)), ((), ())), preferred_element_type=jnp.float32)


def late_kernel(n, keys, block, early, early_rest, middle, middle_rest, out, tile, out_sem):
    w = lax.axis_index("wide")
    snps, size = block.shape[1], middle.shape[0]
    slots = tile.shape[0]

    def out_copy(t):
        chip = (w ^ jnp.where(lax.rem(w, 2) == 0, *keys[t])) // 2
        rows = pl.ds(pl.multiple_of(chip * size, size), size)
        return pltpu.make_async_copy(tile.at[t % slots], out.at[rows], out_sem.at[t % slots])

    for t in range(len(keys)):
        if t >= slots:
            out_copy(t - slots).wait()
        if t < len(keys) - 1:
            rows = pl.ds(t * size, size)
            before, left = early[rows, :], early_rest[rows, :]
        else:
            before, left = middle[...], middle_rest[...]
        product = lax.dot_general(left, block[...], (((1,), (1,)), ((), ())), preferred_element_type=jnp.float32)
        tile[t % slots] = (before + product) / (n * snps)
        out_copy(t).start()
    for t in range(max(len(keys) - slots, 0), len(keys)):
        out_copy(t).wait()


def limit(arrays):
    return min(sum(math.prod(a.shape) * a.dtype.itemsize for a in arrays) + 4 * 2**20, 60 * 2**20)


def multiply(own, near, got, panels, halves, keys):
    n, sub, snps = near.shape
    rows, cols = len(panels) * sub, own.shape[0]
    plan = tuple(key for key in got if key[1] < n - 1)
    width = 256 if cols % 256 == 0 else cols
    scratch = [
        pltpu.VMEM((rows, (n - 1) * snps), jnp.bfloat16),
        pltpu.VMEM((2, rows, width), jnp.float32),
    ]
    operands = [own, near, *[got[key] for key in plan], *panels]
    outs = [
        jax.ShapeDtypeStruct((rows, cols), jnp.float32),
        jax.ShapeDtypeStruct((rows, snps), jnp.bfloat16),
        jax.ShapeDtypeStruct((cols, (n - 1) * snps), jnp.bfloat16),
    ]
    early = pl.pallas_call(
        functools.partial(early_kernel, n, plan),
        out_shape=outs,
        in_specs=[HBM] + [VMEM] * (len(operands) - 1),
        out_specs=[ANY, VMEM, VMEM],
        scratch_shapes=scratch + [pltpu.SemaphoreType.DMA, pltpu.SemaphoreType.DMA((2,))],
        compiler_params=pltpu.CompilerParams(vmem_limit_bytes=limit([*operands[1:], *scratch, *outs[1:]])),
        cost_estimate=pl.CostEstimate(flops=EARLY, bytes_accessed=0, transcendentals=0),
        name="early",
    )(*operands)
    plan = tuple(key for key in got if key[1] >= n // 2)
    operands = [early[2], *halves, *[flip(after(half, early[1]), (1, 1)) for half in halves]]
    outs = [
        jax.ShapeDtypeStruct((2 * sub, cols), jnp.float32),
        jax.ShapeDtypeStruct((2 * sub, snps), jnp.bfloat16),
    ]
    scratch = [pltpu.VMEM((2 * sub, (n - 1) * snps), jnp.bfloat16)]
    middle = pl.pallas_call(
        functools.partial(middle_kernel, n),
        out_shape=outs,
        scratch_shapes=scratch,
        compiler_params=pltpu.CompilerParams(vmem_limit_bytes=limit([*operands, *scratch, *outs])),
        cost_estimate=pl.CostEstimate(flops=MIDDLE, bytes_accessed=0, transcendentals=0),
        name="middle",
    )(*operands)
    operands = [after(near, middle[1]), *[got[key] for key in plan]]
    block = pl.pallas_call(
        functools.partial(last_block_kernel, n, plan),
        out_shape=jax.ShapeDtypeStruct((cols, snps), jnp.bfloat16),
        compiler_params=pltpu.CompilerParams(vmem_limit_bytes=limit(operands)),
        name="last_block",
    )(*operands)
    operands = [block, *early[:2], *middle]
    slots = min(4, len(keys))
    scratch = [pltpu.VMEM((slots, 2 * sub, cols), jnp.float32)]
    return pl.pallas_call(
        functools.partial(late_kernel, n, keys),
        out_shape=jax.ShapeDtypeStruct((rows + 2 * sub, cols), jnp.float32),
        in_specs=[VMEM] * len(operands),
        out_specs=ANY,
        scratch_shapes=scratch + [pltpu.SemaphoreType.DMA((slots,))],
        compiler_params=pltpu.CompilerParams(vmem_limit_bytes=limit([*operands, *scratch])),
        name="late",
    )(*operands)


def after(value, *earlier):
    return lax.optimization_barrier((value, *earlier))[0]


def flip(value, masks):
    size = lax.axis_size("wide")
    return lax.ppermute(value, "wide", [(i, i ^ masks[i & 1]) for i in range(size)])


def spread(panel, earlier):
    size = lax.axis_size("wide")
    bits = [1 << b for b in range(1, size.bit_length() - 1)]
    got = {(0, 0): panel}
    for i in range(len(bits)):
        masks = (bits[i], bits[-1 - i])
        for key, value in list(got.items()):
            if any(key):
                value = after(value, *earlier)
            to = key[0] ^ masks[0], key[1] ^ masks[1]
            if to == (size - 2, size - 2):
                half = value.shape[0] // 2
                got[to] = [flip(value[:half], masks), flip(value[half:], masks)]
            else:
                got[to] = flip(value, masks)
    return got


def shards(dosages, allele_counts, called_counts):
    n, wide = lax.axis_size("narrow"), lax.axis_size("wide")
    z, w = lax.axis_index("narrow"), lax.axis_index("wide")
    snps, cols = dosages.shape
    sub = cols // n
    own, panels = standardize(dosages, allele_counts, called_counts, n)
    got = {(swapped, 1): trade(own, swapped, 1) for swapped in range(2)}
    mine = pick(own, sub)
    pieces = [far_swap(after(value, mine) if m > 2 else value, m) for m, value in enumerate(panels, 2)]
    near = stack(mine, got[0, 1], got[1, 1], pieces)
    ready = []
    for step in range(2, n):
        values = hand_on(got[0, step - 1], got[1, step - 1], near, step - 1)
        ready = values if step == min(3, n - 1) else ready
        for swapped, value in enumerate(values):
            got[swapped, step] = trade(value, swapped, step)
    held = spread(near, ready)
    *keys, final = held
    partner = {key: flip(held[key], (1, 1)) for key in keys}
    panels = [array for key in keys for array in (held[key], partner[key[::-1]])]
    result = multiply(own, near, got, panels, held[final], tuple(held))
    return result.reshape(wide, 1, sub, cols)


def solution(mesh):
    return jax.shard_map(
        shards,
        mesh=mesh,
        in_specs=(P("narrow", "wide"), P("narrow"), P("narrow")),
        out_specs=P(None, "narrow", None, "wide"),
        check_vma=False,
    )
```
